512 devices in a mesh: fsdp: 16 (over y, core), dp: 32 (over z, x).
Axes of the slice: x: 4, y: 8, z: 8, core: 2. Of those that a mesh axis runs over, the one named last changes fastest.
Arguments:
- acts: bfloat16 [32, 2048, 64], P('dp', 'fsdp'), may hold values from -6 to 6
- cot: bfloat16 [32, 2048, 14336], P('dp', 'fsdp'), may hold values from -0.125 to 0.125
- error_in: float32 [32, 64, 14336], P('dp', 'fsdp'), may hold values from -6 to 6
- q_warm: float32 [14336, 32], P('fsdp'), may hold values from -0.046875 to 0.046875
- quorum: int32 [32], replicated, may hold values from 0 to 1, as said below
- counts: int32 [32], replicated, may hold values from 1 to 4
Outputs:
- error_out: float32 [32, 64, 14336], P('dp', 'fsdp')
- approx: float32 [64, 14336], P('fsdp', 'dp')
- q_next: float32 [14336, 32], P('fsdp')
The draws below stay inside these ranges and needn't reach their ends.
Inputs may be any that keep to these rules, and one draw needn't show every extreme that they name: At least one island has quorum 1.
All inputs are finite; a program needn't handle non-finite values.
Results may differ from the reference program's by a relative error of at most 0.0004.
Values sent between devices are 32-bit elements; how exact they have to be, the bound alone decides.
No kernel may reach another device: no remote copies, remote signals or barrier semaphores. Data moves between devices by JAX's collectives and lax.ppermute only.
A program may use at most 64 MiB of HBM per device.

```python
import jax
import jax.numpy as jnp
from jax import lax

D_BLK = 64
F_BLK = 14336
RANK = 32
TOK_DEV = 128
TOK_GROUP = 2048
N_FSDP = 16
N_DP = 32


def draw_quorum(key, part):
    key = jax.random.fold_in(key, 7)
    key_bits, key_forced = jax.random.split(key)
    bits = jax.random.randint(key_bits, (N_DP,), 0, 4)
    present = (bits > 0).astype(jnp.int32)
    forced = jax.random.randint(key_forced, (), 0, N_DP)
    chosen = (jnp.arange(N_DP) == forced).astype(jnp.int32)
    return jnp.maximum(present, chosen)


def plant(result, own_key, low, largest):
    dims = result.shape
    index_at = [jax.random.randint(jax.random.fold_in(own_key, axis), (), 0, dims[axis]) for axis in range(len(dims))]
    result = result.at[tuple(index_at)].set(low)
    longest = dims.index(max(dims))
    index_at[longest] = (index_at[longest] + 1) % dims[longest]
    return result.at[tuple(index_at)].set(largest)


def level_of(key, shape, cuts, smallest, largest):
    loudness, own = 1.0, jax.random.fold_in(key, 6)
    for dim, shards_of in cuts:
        draws = jnp.exp(jax.random.uniform(jax.random.fold_in(own, dim), (shards_of,), jnp.float32, smallest / len(cuts), largest / len(cuts)))
        loudness = loudness * jnp.repeat(draws, shape[dim] // shards_of).reshape([-1 if axis == dim else 1 for axis in range(len(shape))])
    return loudness


def bell_draw(key, extent, deviation, reach, shards=(), kind=jnp.bfloat16):
    gain = level_of(key, extent, shards, -0.22, 0.18) if shards else 1.0
    values = jax.random.normal(key, extent, jnp.float32) * deviation * gain
    return jnp.minimum(jnp.maximum(values, -reach), reach).astype(kind)


def setup_inputs(seed: int = 0) -> dict:
    key_list = jax.random.split(jax.random.key(seed), 7)
    acts = bell_draw(key_list[0], (N_DP, TOK_GROUP, D_BLK), 1.0, 6.0, ((0, 32), (1, 16)))
    cot = bell_draw(key_list[1], (N_DP, TOK_GROUP, F_BLK), (TOK_DEV * N_FSDP) ** -0.5, 0.125, ((0, 32), (1, 16)))
    error_in = bell_draw(key_list[2], (N_DP, D_BLK, F_BLK), 0.5, 6.0, ((0, 32), (1, 16)), jnp.float32)
    q_warm = bell_draw(key_list[3], (F_BLK, RANK), F_BLK ** -0.5, 0.046875, ((0, 16),), jnp.float32)
    quorum = draw_quorum(jax.random.fold_in(key_list[6], 71), 0)
    counts = plant(jax.random.randint(key_list[5], (N_DP,), 1, 5), jax.random.fold_in(key_list[5], 1), 1, 4).astype(jnp.int32)
    return {"acts": acts, "cot": cot, "error_in": error_in, "q_warm": q_warm, "quorum": quorum, "counts": counts}


def island_gradient(pair):
    acts_one, cot_one = pair
    acts_groups = acts_one.reshape(N_FSDP, TOK_DEV, D_BLK)
    cot_groups = cot_one.reshape(N_FSDP, TOK_DEV, F_BLK)

    def add_group(running, piece):
        partial_value = jnp.dot(piece[0].T.astype(jnp.float32), piece[1].astype(jnp.float32), preferred_element_type=jnp.float32)
        return (running + partial_value, None)
    running, _ = lax.scan(add_group, jnp.zeros((D_BLK, F_BLK), jnp.float32), (acts_groups, cot_groups))
    return running

def reference(acts, cot, error_in, q_warm, quorum, counts):
    highest = lax.Precision.HIGHEST
    gradient = lax.map(island_gradient, (acts, cot))
    merged = gradient + error_in
    weight = (quorum * counts).astype(jnp.float32)
    total = jnp.sum(weight)
    p_all = jnp.einsum('idf,fr->idr', merged, q_warm, precision=highest)
    p_sum = jnp.einsum('i,idr->dr', weight, p_all, precision=highest) / total
    gram = jnp.dot(p_sum.T, p_sum, precision=highest)
    lower = jnp.linalg.cholesky(gram)
    p_hat = jax.scipy.linalg.solve_triangular(lower, p_sum.T, lower=True).T
    q_all = jnp.einsum('idf,dr->ifr', merged, p_hat, precision=highest)
    q_next = jnp.einsum('i,ifr->fr', weight, q_all, precision=highest) / total
    approx = jnp.dot(p_hat, q_next.T, precision=highest)
    error_out = merged - approx[None]
    return (error_out, approx, q_next)
```

```python
import jax
import jax.numpy as jnp
from jax import lax
from jax.sharding import PartitionSpec as P

HIGHEST = lax.Precision.HIGHEST


def shards(acts, cot, error_in, q_warm, quorum, counts):
    groups = lax.axis_size("fsdp")
    islands = lax.axis_size("dp")
    chips = groups // 2
    f = lax.axis_index("fsdp")
    i = lax.axis_index("dp")
    y, core = f // 2, f % 2
    a, c = acts[0], cot[0]
    rank = q_warm.shape[1]
    d_blk, f_blk = a.shape[1], c.shape[1]
    rows = d_blk // groups
    chunk = 2 * rows
    half = chips // 2
    cols = f_blk // islands
    piece = f_blk // (groups * islands)

    whole_q = lax.all_gather(q_warm, "fsdp", axis=0, tiled=True)

    weight = (quorum * counts).astype(jnp.float32)
    total = jnp.sum(weight)
    mine = jnp.sum(jnp.where(jnp.arange(islands) == i, weight, 0.0)) / total

    up = [y + d for d in range(half - 1, 0, -1)] + [y + half]
    down = [y - d for d in range(half - 1, 0, -1)] + [y]
    order = jnp.where(core == 0, jnp.stack(up + down), jnp.stack(down + up)) % chips
    picked = (order[:, None] * chunk + jnp.arange(chunk)[None, :]).reshape(-1)
    onehot = (picked[None, :] == jnp.arange(d_blk)[:, None]).astype(a.dtype)
    chosen = jnp.dot(a, onehot, preferred_element_type=jnp.float32).astype(a.dtype)
    other = jnp.einsum("td,tf->df", chosen[:, d_blk // 2 :], c, preferred_element_type=jnp.float32)
    swap = [(k, k ^ 1) for k in range(groups)]
    got = lax.ppermute(other, "fsdp", swap)
    own = jnp.einsum("td,tf->df", chosen[:, : d_blk // 2], c, preferred_element_type=jnp.float32)
    both = (own + got).reshape(half, chunk, f_blk)

    ring = [(2 * k, 2 * ((k + 1) % chips)) for k in range(chips)] + [(2 * k + 1, 2 * ((k - 1) % chips) + 1) for k in range(chips)]
    run = lax.ppermute(both[half - 1], "fsdp", ring)
    run = jnp.where(core == 0, run, 0.0)
    for k in range(half - 1):
        run = lax.ppermute(run + both[k], "fsdp", ring)
    run = run + jnp.where(core == 1, both[half - 1], 0.0)
    share = run + lax.ppermute(run, "fsdp", swap)
    share = lax.dynamic_slice_in_dim(share, core * rows, rows, 0)
    merged = share + error_in[0]

    p_rows = jnp.dot(merged, whole_q, precision=HIGHEST)
    sent = merged.reshape(rows, islands, cols).transpose(1, 0, 2)
    sent = jnp.concatenate([sent, jnp.broadcast_to(p_rows[None], (islands, rows, rank))], axis=2) * mine
    mean_rows = jnp.sum(lax.all_to_all(sent, "dp", 0, 0, tiled=True), axis=0)
    width = cols + rank
    sent = jnp.broadcast_to(mean_rows[None], (groups, rows, width))
    mean = lax.all_to_all(sent, "fsdp", 0, 0, tiled=True).reshape(d_blk, width)
    mean_m, p_sum = mean[:, :cols], mean[:, cols:]

    part = islands // 2
    moves = []
    for g in range(groups):
        for k in range(islands):
            moves.append((g * islands + k, (k // 2) * islands + (k % 2) * part + g))
    m_piece = lax.dynamic_slice_in_dim(mean_m, f * piece, piece, 1)
    m_piece = lax.ppermute(m_piece, ("fsdp", "dp"), moves)

    gram = jnp.dot(p_sum.T, p_sum, precision=HIGHEST)
    lower = jnp.linalg.cholesky(gram)
    p_hat = jax.scipy.linalg.solve_triangular(lower, p_sum.T, lower=True).T

    q_cols = jnp.dot(p_hat.T, mean_m, precision=HIGHEST)
    p_own = lax.dynamic_slice_in_dim(p_hat, f * rows, rows, 0)
    approx = jnp.dot(p_own, q_cols, precision=HIGHEST)
    q_piece = jnp.dot(p_hat.T, m_piece, precision=HIGHEST)
    extra = rank * piece // rows
    sent = jnp.concatenate([approx, q_piece.reshape(rows, extra)], axis=1)
    sent = jnp.broadcast_to(sent[None], (islands, rows, cols + extra))
    got = lax.all_to_all(sent, "dp", 0, 0, tiled=True)
    approx_rows = got[:, :, :cols].transpose(1, 0, 2).reshape(rows, f_blk)
    q_next = got[:, :, cols:].reshape(islands, rank, piece).transpose(0, 2, 1).reshape(islands * piece, rank)
    error_out = (merged - approx_rows)[None]
    return (error_out, approx, q_next)


def solution(mesh):
    return jax.shard_map(
        shards,
        mesh=mesh,
        in_specs=(
            P("dp", "fsdp", None),
            P("dp", "fsdp", None),
            P("dp", "fsdp", None),
            P("fsdp", None),
            P(),
            P(),
        ),
        out_specs=(P("dp", "fsdp", None), P("fsdp", "dp"), P("fsdp", None)),
        check_vma=False,
    )
```

```python
import functools

import jax
import jax.numpy as jnp
from jax import lax
from jax.experimental import pallas as pl
from jax.experimental.pallas import tpu as pltpu
from jax.sharding import PartitionSpec as P

HIGHEST = lax.Precision.HIGHEST
LANES = 128
SLOT = 32
F32 = jnp.float32


def iota(shape, axis):
    return lax.broadcasted_iota(jnp.int32, shape, axis)


def contract(x, z, dims):
    return lax.dot_general(x, z, ((dims[:1], dims[1:]), ((), ())), precision=HIGHEST, preferred_element_type=F32)


def pack_kernel(n_dp, piece, where_ref, mine_ref, own_ref, got_ref, q_ref, *refs):
    *shard_refs, sent_ref, merged_ref, chip_ref = refs
    y, core = where_ref[0], where_ref[1]
    chips, span = len(shard_refs) + 1, q_ref.shape[1]
    mid = merged_ref.shape[1]
    chip_ref[...] = own_ref[...] + got_ref[...]

    rank = q_ref.shape[0]
    parts = jnp.zeros((8, rank), F32)
    for k in range(chips):
        if k == 0:
            shard, chip = q_ref[...], y
        else:
            held = shard_refs[k - 1][...]
            shard = jnp.concatenate([held[:, a * span : (a + 1) * span] for a in range(rank // 8)], axis=0)
            step = k if k <= chips // 2 else k - chips // 2
            back = (core == 0) if k <= chips // 2 else (core == 1)
            chip = lax.rem(y + jnp.where(back, chips - step, step), chips)
        start = pl.multiple_of((2 * chip + core) * span, LANES)
        parts = parts + contract(chip_ref[:, pl.ds(start, span)], shard, (1, 1))

    left, right = chip_ref[:, :mid], chip_ref[:, mid:]
    low = iota((8, mid), 0) < 4
    upper = jnp.where(low, left, pltpu.roll(right, 4, 0))
    lower = jnp.where(low, pltpu.roll(left, 4, 0), right)
    merged = jnp.where(core == 0, upper, lower)
    merged_ref[...] = merged
    mine = mine_ref[0]
    scaled = merged * mine

    slots = mid // span
    width = slots * SLOT
    spot = (iota((rank, width), 1) // SLOT) * (SLOT - piece) + iota((rank, width), 1) % SLOT - piece
    place = ((iota((rank, width), 1) % SLOT >= piece) & (spot == iota((rank, width), 0))).astype(F32)
    base = contract(parts * mine, place, (1, 0))
    lane = iota((8, LANES), 1)
    for k in range(n_dp):
        first = (k * piece) // LANES
        for v in range(width // LANES):
            out = base[:, v * LANES : (v + 1) * LANES]
            for b in range(LANES // SLOT):
                f = v * (LANES // SLOT) + b
                for w in range(first, (k * piece + piece - 1) // LANES + 1):
                    src = f * span + w * LANES
                    at = k * piece - w * LANES
                    moved = pltpu.roll(scaled[:, src : src + LANES], (b * SLOT - at) % LANES, 1)
                    lo = b * SLOT + max(0, -at)
                    hi = b * SLOT + min(piece, LANES - at)
                    out = jnp.where((lane >= lo) & (lane < hi), moved, out)
            sent_ref[k, :, v * LANES : (v + 1) * LANES] = out


def factor_kernel(piece, where_ref, mean_ref, sent_ref):
    f = where_ref[0]
    groups, _, width = mean_ref.shape
    slots = width // SLOT
    rank = slots * (SLOT - piece)
    d_blk = groups * 4
    mean = mean_ref[...].reshape(groups * 8, width)
    lane_i, sub_i = iota((width, LANES), 0), iota((width, LANES), 1)
    pick = ((lane_i % SLOT >= piece) & ((lane_i // SLOT) * (SLOT - piece) + lane_i % SLOT - piece == sub_i)).astype(F32)
    p_all = contract(mean, pick, (1, 0)).reshape(groups // 2, 2, 8, LANES)
    p_sum = (p_all[:, 0] + p_all[:, 1]).reshape(d_blk, LANES)

    sub, lane = iota((d_blk, LANES), 0), iota((d_blk, LANES), 1)
    wide = p_sum + (lane == sub + rank).astype(F32)
    a = contract(p_sum, wide, (0, 0))[:rank]
    row_i = iota((rank, LANES), 0)
    for k in range(rank):
        pivot = a[k : k + 1, k : k + 1]
        inv = lax.rsqrt(pivot)
        inv = inv * (1.5 - 0.5 * pivot * inv * inv)
        row = a[k : k + 1, :] * inv
        col = jnp.where(row_i[:, :1] > k, a[:, k : k + 1] * inv, 0.0)
        a = jnp.where(row_i == k, row, a - col * row)

    approx = jnp.zeros((8, width), F32)
    halves = []
    src, dst = iota((LANES, groups * 8), 0) - rank, iota((LANES, groups * 8), 1)
    for h in range(2):
        spread = ((dst % 8 // 4 == h) & (src == dst // 8 * 4 + dst % 4)).astype(F32)
        q_half = contract(contract(a, spread, (1, 0)), mean, (1, 0))
        own = ((iota((LANES, 8), 1) // 4 == h) & (iota((LANES, 8), 0) - rank == f * 4 + iota((LANES, 8), 1) % 4)).astype(F32)
        approx = approx + contract(contract(a, own, (1, 0)), q_half, (0, 0))
        halves.append(q_half)
    q_mine = jnp.where(f < slots, halves[0], halves[1])
    q_mine = pltpu.roll(q_mine, lax.rem(width - lax.rem(f, slots) * SLOT, width), 1)[:, :LANES]
    lane = iota((8, LANES), 1)
    q_out = jnp.zeros((8, LANES), F32)
    for b in range(rank // 8):
        q_out = jnp.where(lane // SLOT == b, pltpu.roll(q_mine[b * 8 : b * 8 + 8], b * SLOT, 1), q_out)
    for k in range(sent_ref.shape[0]):
        sent_ref[k, :, :width] = approx
        sent_ref[k, :, width:] = q_out


def unpack_kernel(piece, where_ref, got_ref, merged_ref, error_ref, approx_ref, q_ref, whole_ref):
    i = where_ref[0]
    n_dp, _, width = got_ref.shape
    width -= LANES
    mid = merged_ref.shape[1]
    span = q_ref.shape[1]
    slots = width // SLOT
    lane = iota((8, LANES), 1)
    for f in range(slots):
        v, b = f * SLOT // LANES, f % (LANES // SLOT)
        for w in range(span // LANES):
            out = jnp.zeros((8, LANES), F32)
            for k in range(w * LANES // piece, ((w + 1) * LANES - 1) // piece + 1):
                at = k * piece - w * LANES
                moved = pltpu.roll(got_ref[k, :, v * LANES : (v + 1) * LANES], (at - b * SLOT) % LANES, 1)
                out = jnp.where((lane >= at) & (lane < at + piece), moved, out)
            whole_ref[:, f * span + w * LANES : f * span + (w + 1) * LANES] = out
    for b in range(q_ref.shape[0] // 8):
        for w in range(span // LANES):
            out = jnp.zeros((8, LANES), F32)
            for k in range(w * LANES // piece, ((w + 1) * LANES - 1) // piece + 1):
                at = k * piece - w * LANES
                moved = pltpu.roll(got_ref[k, :, width:], (at - b * SLOT) % LANES, 1)
                out = jnp.where((lane >= at) & (lane < at + piece), moved, out)
            q_ref[b * 8 : b * 8 + 8, w * LANES : (w + 1) * LANES] = out
    error = merged_ref[...] - whole_ref[...]
    error_ref[:, :mid] = error[:4]
    error_ref[:, mid:] = error[4:]
    cols = approx_ref.shape[1]
    per_half = mid // cols
    at = lax.rem(i, per_half) * cols
    start = pl.multiple_of(at // LANES * LANES, LANES)
    window = whole_ref[:, pl.ds(start, cols + LANES // 2)]
    window = jnp.where(lax.rem(at, LANES) == 0, window, pltpu.roll(window, cols, 1))
    window = jnp.where(i < per_half, window[:4], window[4:])
    approx_ref[...] = window[:, :cols]


VMEM = pl.BlockSpec(memory_space=pltpu.VMEM)
SMEM = pl.BlockSpec(memory_space=pltpu.SMEM)
PARAMS = pltpu.CompilerParams(vmem_limit_bytes=24 * 2**20)


def shards(acts, cot, error_in, q_warm, quorum, counts):
    groups = lax.axis_size("fsdp")
    islands = lax.axis_size("dp")
    chips = groups // 2
    f = lax.axis_index("fsdp")
    i = lax.axis_index("dp")
    y, core = f // 2, f % 2
    a, c = acts[0], cot[0]
    own_q, rank = q_warm.shape
    d_blk, f_blk = a.shape[1], c.shape[1]
    rows = d_blk // groups
    chunk = 2 * rows
    half = chips // 2
    cols = f_blk // islands
    piece = own_q // islands
    mid = f_blk // 2

    weight = (quorum * counts).astype(F32)
    total = jnp.sum(weight)
    mine = jnp.sum(jnp.where(jnp.arange(islands) == i, weight, 0.0)) / total

    up = [y + d for d in range(half - 1, 0, -1)] + [y + half]
    down = [y - d for d in range(half - 1, 0, -1)] + [y]
    order = jnp.where(core == 0, jnp.stack(up + down), jnp.stack(down + up)) % chips
    picked = (order[:, None] * chunk + jnp.arange(chunk)[None, :]).reshape(-1)
    onehot = (picked[None, :] == jnp.arange(d_blk)[:, None]).astype(a.dtype)
    chosen = jnp.dot(a, onehot, preferred_element_type=F32).astype(a.dtype)
    first, second = chosen[:, : d_blk // 2], chosen[:, d_blk // 2 :]

    def product(x, z):
        return jnp.einsum("td,tf->df", x, z, preferred_element_type=F32)

    swap = [(k, k ^ 1) for k in range(groups)]
    rise = [(2 * k, 2 * ((k + 1) % chips)) for k in range(chips)] + [(2 * k + 1, 2 * ((k - 1) % chips) + 1) for k in range(chips)]
    fall = [(2 * k, 2 * ((k - 1) % chips)) for k in range(chips)] + [(2 * k + 1, 2 * ((k + 1) % chips) + 1) for k in range(chips)]
    rings = (rise, fall)
    rising = (core == 0, core == 1)

    q_t = q_warm.T
    held = q_t.reshape(rank // 8, 8, own_q).transpose(1, 0, 2).reshape(8, rank // 8 * own_q)
    both, run, shards_q = [], [], [[], []]
    for x, other, z in ((first, second, c[:, :mid]), (second, first, c[:, mid:])):
        got = lax.ppermute(product(other, z), "fsdp", swap)
        both.append((product(x, z) + got).reshape(half, chunk, mid))
    run = [lax.ppermute(jnp.concatenate([both[s][half - 1], held], axis=1), "fsdp", rings[s]) for s in range(2)]
    for k in range(half):
        for s in range(2):
            if run[s].shape[1] > mid:
                shards_q[s].append(run[s][:, mid:])
                run[s] = run[s][:, :mid]
            if k == 0:
                run[s] = jnp.where(rising[s], run[s], 0.0)
        if k < half - 1:
            for s in range(2):
                nxt = run[s] + both[s][k]
                if len(shards_q[s]) < half - s:
                    nxt = jnp.concatenate([nxt, shards_q[s][-1]], axis=1)
                run[s] = lax.ppermute(nxt, "fsdp", rings[s])
    place = (jnp.arange(chunk) // rows == core).astype(F32)[:, None]
    errors = jnp.concatenate([error_in[0], error_in[0]], axis=0) * place
    run = [run[s] + jnp.where(rising[s], 0.0, both[s][half - 1]) for s in range(2)]
    run = jnp.concatenate(run, axis=1) + errors
    got = lax.ppermute(run, "fsdp", swap)

    width = mid // own_q * SLOT
    sent, merged = pl.pallas_call(
        functools.partial(pack_kernel, islands, piece),
        out_shape=(jax.ShapeDtypeStruct((islands, 8, width), F32), jax.ShapeDtypeStruct((8, mid), F32)),
        in_specs=[SMEM, SMEM] + [VMEM] * (3 + chips - 1),
        out_specs=(VMEM, VMEM),
        scratch_shapes=[pltpu.VMEM((8, f_blk), F32)],
        compiler_params=PARAMS,
        name="pack",
    )(jnp.stack([y, core]), mine[None], run, got, q_t, *shards_q[0], *shards_q[1])
    mean = jnp.sum(lax.all_to_all(sent, "dp", 0, 0, tiled=True), axis=0)
    mean = lax.all_to_all(jnp.broadcast_to(mean[None], (groups, 8, width)), "fsdp", 0, 0, tiled=True)
    sent = pl.pallas_call(
        functools.partial(factor_kernel, piece),
        out_shape=jax.ShapeDtypeStruct((islands, 8, width + LANES), F32),
        in_specs=[SMEM, VMEM],
        out_specs=VMEM,
        compiler_params=PARAMS,
        name="factor",
    )(f[None], mean)
    got = lax.all_to_all(sent, "dp", 0, 0, tiled=True)
    error_out, approx, q_next = pl.pallas_call(
        functools.partial(unpack_kernel, piece),
        out_shape=(
            jax.ShapeDtypeStruct((rows, f_blk), F32),
            jax.ShapeDtypeStruct((rows, cols), F32),
            jax.ShapeDtypeStruct((rank, own_q), F32),
        ),
        in_specs=[SMEM, VMEM, VMEM],
        out_specs=(VMEM, VMEM, VMEM),
        scratch_shapes=[pltpu.VMEM((8, mid), F32)],
        compiler_params=PARAMS,
        name="unpack",
    )(i[None], got, merged)
    return (error_out[None], approx, q_next.T)


def solution(mesh):
    return jax.shard_map(
        shards,
        mesh=mesh,
        in_specs=(
            P("dp", "fsdp", None),
            P("dp", "fsdp", None),
            P("dp", "fsdp", None),
            P("fsdp", None),
            P(),
            P(),
        ),
        out_specs=(P("dp", "fsdp", None), P("fsdp", "dp"), P("fsdp", None)),
        check_vma=False,
    )
```

```python
import functools

import jax
import jax.numpy as jnp
from jax import lax
from jax.experimental import pallas as pl
from jax.experimental.pallas import tpu as pltpu
from jax.sharding import PartitionSpec as P

HIGHEST = lax.Precision.HIGHEST
LANES = 128
SLOT = 32
F32 = jnp.float32


def iota(shape, axis):
    return lax.broadcasted_iota(jnp.int32, shape, axis)


def contract(x, z, dims):
    return lax.dot_general(x, z, ((dims[:1], dims[1:]), ((), ())), precision=HIGHEST, preferred_element_type=F32)


def product_kernel(splits, where_ref, a_ref, c_ref, error_ref, *refs):
    *out_refs, held_ref, sems = refs
    side = where_ref[0]
    span = error_ref.shape[1] // (2 * sems.shape[0])
    starts = [pl.multiple_of((2 * j + side) * span, LANES) for j in range(sems.shape[0])]
    copies = []
    for j, at in enumerate(starts):
        copies.append(pltpu.make_async_copy(c_ref.at[:, pl.ds(at, span)], held_ref.at[:, j * span : (j + 1) * span], sems.at[j]))
        copies[j].start()
    chunk = error_ref.shape[0]
    a = a_ref[...]
    for j in range(0, len(copies), 2):
        copies[j].wait()
        copies[j + 1].wait()
        cols = slice(j * span, (j + 2) * span)
        out = jnp.dot(a, held_ref[:, cols], preferred_element_type=F32)
        last = out[-chunk:] + jnp.concatenate([error_ref[:, pl.ds(at, span)] for at in starts[j : j + 2]], axis=1)
        first = 0
        for n, size in enumerate(splits):
            if n < len(splits) - 1:
                out_refs[n][:, cols] = out[first : first + size]
            else:
                if size > chunk:
                    out_refs[n][: size - chunk, cols] = out[first : first + size - chunk]
                out_refs[n][size - chunk :, cols] = last
            first += size


def pack_kernel(n_dp, piece, where_ref, mine_ref, long_ref, short_ref, own_ref, q_ref, *refs):
    *shard_refs, sent_ref, kept_ref, given_ref, sum_ref = refs
    y, core = where_ref[0], where_ref[1]
    chips, span = len(shard_refs) + 1, q_ref.shape[1]
    mid = own_ref.shape[1]
    total = long_ref[:, :mid] + short_ref[:, :mid] + own_ref[...]
    sum_ref[...] = total
    upper, lower = total[:4], total[4:]
    kept_ref[...] = jnp.where(core == 0, upper, lower)
    given_ref[...] = jnp.where(core == 0, lower, upper)

    rank = q_ref.shape[0]
    parts = jnp.zeros((8, rank), F32)
    for k in range(chips):
        if k == 0:
            shard, chip = q_ref[...], y
        else:
            held = shard_refs[k - 1][:, mid:]
            shard = jnp.concatenate([held[:, a * span : (a + 1) * span] for a in range(rank // 8)], axis=0)
            step = k if k <= chips // 2 else chips // 2 - k
            chip = lax.rem(y + chips - jnp.where(core == 0, step, -step), chips)
        start = pl.multiple_of(chip * span, LANES)
        parts = parts + contract(sum_ref[:, pl.ds(start, span)], shard, (1, 1))

    mine = mine_ref[0]
    scaled = total * mine

    slots = mid // span
    width = slots * SLOT
    spot = (iota((rank, width), 1) // SLOT) * (SLOT - piece) + iota((rank, width), 1) % SLOT - piece
    place = ((iota((rank, width), 1) % SLOT >= piece) & (spot == iota((rank, width), 0))).astype(F32)
    base = contract(parts * mine, place, (1, 0))
    lane = iota((8, LANES), 1)
    for k in range(n_dp):
        first = (k * piece) // LANES
        for v in range(width // LANES):
            out = base[:, v * LANES : (v + 1) * LANES]
            for b in range(LANES // SLOT):
                f = v * (LANES // SLOT) + b
                for w in range(first, (k * piece + piece - 1) // LANES + 1):
                    src = f * span + w * LANES
                    at = k * piece - w * LANES
                    moved = pltpu.roll(scaled[:, src : src + LANES], (b * SLOT - at) % LANES, 1)
                    lo = b * SLOT + max(0, -at)
                    hi = b * SLOT + min(piece, LANES - at)
                    out = jnp.where((lane >= lo) & (lane < hi), moved, out)
            sent_ref[k, :, v * LANES : (v + 1) * LANES] = out


def factor_kernel(piece, where_ref, mean_ref, sent_ref):
    f = where_ref[3]
    groups, _, width = mean_ref.shape
    slots = width // SLOT
    rank = slots * (SLOT - piece)
    d_blk = groups * 4
    mean = mean_ref[...].reshape(groups * 8, width)
    lane_i, sub_i = iota((width, LANES), 0), iota((width, LANES), 1)
    pick = ((lane_i % SLOT >= piece) & ((lane_i // SLOT) * (SLOT - piece) + lane_i % SLOT - piece == sub_i)).astype(F32)
    p_all = contract(mean, pick, (1, 0)).reshape(groups // 2, 2, 8, LANES)
    p_sum = (p_all[:, 0] + p_all[:, 1]).reshape(d_blk, LANES)

    sub, lane = iota((d_blk, LANES), 0), iota((d_blk, LANES), 1)
    wide = p_sum + (lane == sub + rank).astype(F32)
    a = contract(p_sum, wide, (0, 0))[:rank]
    row_i = iota((rank, LANES), 0)
    for k in range(rank):
        pivot = a[k : k + 1, k : k + 1]
        inv = lax.rsqrt(pivot)
        inv = inv * (1.5 - 0.5 * pivot * inv * inv)
        row = a[k : k + 1, :] * inv
        col = jnp.where(row_i[:, :1] > k, a[:, k : k + 1] * inv, 0.0)
        a = jnp.where(row_i == k, row, a - col * row)

    approx = jnp.zeros((8, width), F32)
    halves = []
    src, dst = iota((LANES, groups * 8), 0) - rank, iota((LANES, groups * 8), 1)
    for h in range(2):
        spread = ((dst // 8 % 2 == h) & (src == dst // 16 * 8 + dst % 8)).astype(F32)
        q_half = contract(contract(a, spread, (1, 0)), mean, (1, 0))
        own = ((iota((LANES, 8), 1) // 4 == h) & (iota((LANES, 8), 0) - rank == f * 4 + iota((LANES, 8), 1) % 4)).astype(F32)
        approx = approx + contract(contract(a, own, (1, 0)), q_half, (0, 0))
        halves.append(q_half)
    q_mine = jnp.where(lax.rem(f, 2) == 0, halves[0], halves[1])
    q_mine = pltpu.roll(q_mine, lax.rem(width - f // 2 * SLOT, width), 1)[:, :LANES]
    lane = iota((8, LANES), 1)
    q_out = jnp.zeros((8, LANES), F32)
    for b in range(rank // 8):
        q_out = jnp.where(lane // SLOT == b, pltpu.roll(q_mine[b * 8 : b * 8 + 8], b * SLOT, 1), q_out)
    for k in range(sent_ref.shape[0]):
        sent_ref[k, :, :width] = approx
        sent_ref[k, :, width:] = q_out


def unpack_kernel(piece, where_ref, got_ref, kept_ref, got_row_ref, error_ref, approx_ref, q_ref, whole_ref):
    i, core = where_ref[2], where_ref[1]
    n_dp, _, width = got_ref.shape
    width -= LANES
    span = q_ref.shape[1]
    slots = width // SLOT
    lane = iota((8, LANES), 1)
    for f in range(slots):
        v, b = f * SLOT // LANES, f % (LANES // SLOT)
        for w in range(span // LANES):
            out = jnp.zeros((8, LANES), F32)
            for k in range(w * LANES // piece, ((w + 1) * LANES - 1) // piece + 1):
                at = k * piece - w * LANES
                moved = pltpu.roll(got_ref[k, :, v * LANES : (v + 1) * LANES], (at - b * SLOT) % LANES, 1)
                out = jnp.where((lane >= at) & (lane < at + piece), moved, out)
            whole_ref[:, f * span + w * LANES : f * span + (w + 1) * LANES] = out
    for b in range(q_ref.shape[0] // 8):
        for w in range(span // LANES):
            out = jnp.zeros((8, LANES), F32)
            for k in range(w * LANES // piece, ((w + 1) * LANES - 1) // piece + 1):
                at = k * piece - w * LANES
                moved = pltpu.roll(got_ref[k, :, width:], (at - b * SLOT) % LANES, 1)
                out = jnp.where((lane >= at) & (lane < at + piece), moved, out)
            q_ref[b * 8 : b * 8 + 8, w * LANES : (w + 1) * LANES] = out
    for f in range(2 * slots):
        h, at = f % 2, f // 2 * span
        merged = jnp.where(core == h, kept_ref[:, at : at + span], got_row_ref[:, at : at + span])
        error_ref[:, f * span : (f + 1) * span] = merged - whole_ref[4 * h : 4 * h + 4, at : at + span]
    cols = approx_ref.shape[1]
    f, odd = i // 2, lax.rem(i, 2)
    start = pl.multiple_of(f // 2 * span + odd * (cols // LANES * LANES), LANES)
    window = whole_ref[:, pl.ds(start, cols + LANES // 2)]
    window = jnp.where(odd == 0, window, pltpu.roll(window, cols, 1))
    window = jnp.where(lax.rem(f, 2) == 0, window[:4], window[4:])
    approx_ref[...] = window[:, :cols]


VMEM = pl.BlockSpec(memory_space=pltpu.VMEM)
SMEM = pl.BlockSpec(memory_space=pltpu.SMEM)
PARAMS = pltpu.CompilerParams(vmem_limit_bytes=8 * 2**20)


def shards(acts, cot, error_in, q_warm, quorum, counts):
    groups = lax.axis_size("fsdp")
    islands = lax.axis_size("dp")
    chips = groups // 2
    f = lax.axis_index("fsdp")
    i = lax.axis_index("dp")
    y, core = f // 2, f % 2
    a, c = acts[0], cot[0]
    own_q, rank = q_warm.shape
    d_blk, f_blk = a.shape[1], c.shape[1]
    rows = d_blk // groups
    chunk = 2 * rows
    half = chips // 2
    cols = f_blk // islands
    piece = own_q // islands
    mid = f_blk // 2

    weight = (quorum * counts).astype(F32)
    total = jnp.sum(weight)
    mine = jnp.sum(jnp.where(jnp.arange(islands) == i, weight, 0.0)) / total

    swap = [(k, k ^ 1) for k in range(groups)]
    rise = [(2 * k, 2 * ((k + 1) % chips)) for k in range(chips)] + [(2 * k + 1, 2 * ((k - 1) % chips) + 1) for k in range(chips)]
    fall = [(k, j) for j, k in rise]
    where = jnp.stack([y, core, i, f])
    block = jnp.arange(d_blk) // chunk
    ahead = jnp.where(block < half, half - block, block - (chips - 1))

    place = jnp.arange(chunk)[:, None] // rows == core
    errors = jnp.where(place, jnp.concatenate([error_in[0], error_in[0]], axis=0), 0.0)

    def product(side, splits):
        picked = (y + jnp.where(side == 0, ahead, -ahead)) % chips * chunk + jnp.arange(d_blk) % chunk
        onehot = (picked[:, None] == jnp.arange(d_blk)[None, :]).astype(a.dtype)
        chosen = jnp.einsum("nd,td->nt", onehot, a, preferred_element_type=F32).astype(a.dtype)
        return pl.pallas_call(
            functools.partial(product_kernel, splits),
            out_shape=[jax.ShapeDtypeStruct((size, mid), F32) for size in splits],
            in_specs=[SMEM, VMEM, pl.BlockSpec(memory_space=pl.ANY), VMEM],
            out_specs=[VMEM] * len(splits),
            scratch_shapes=[pltpu.VMEM((c.shape[0], mid), c.dtype), pltpu.SemaphoreType.DMA((chips,))],
            compiler_params=pltpu.CompilerParams(vmem_limit_bytes=6 * 2**20),
            name="product",
        )(side[None], chosen, c, errors)

    other_long, other_short = product(1 - core, (half * chunk, half * chunk))
    far, *own = product(core, (chunk,) * chips)
    got_long = lax.ppermute(other_long, "fsdp", swap)
    got_short = lax.ppermute(other_short, "fsdp", swap)
    far = far + got_long[:chunk]
    long = [own[k] + got_long[(k + 1) * chunk : (k + 2) * chunk] for k in range(half - 1)]
    short = [own[half - 1 + k] + got_short[k * chunk : (k + 1) * chunk] for k in range(half)]

    q_t = q_warm.T
    held = q_t.reshape(rank // 8, 8, own_q).transpose(1, 0, 2).reshape(8, rank // 8 * own_q)
    run_long = [lax.ppermute(jnp.concatenate([far, held], axis=1), "fsdp", rise)]
    run_short = []
    for k in range(half - 1):
        last = run_long[-1]
        run_long.append(lax.ppermute(jnp.concatenate([last[:, :mid] + long[k], last[:, mid:]], axis=1), "fsdp", rise))
        if k == 0:
            last = jnp.concatenate([short[0], held], axis=1)
        else:
            last = jnp.concatenate([run_short[-1][:, :mid] + short[k], run_short[-1][:, mid:]], axis=1)
        run_short.append(lax.ppermute(last, "fsdp", fall))

    width = mid // own_q * SLOT
    sent, kept, given = pl.pallas_call(
        functools.partial(pack_kernel, islands, piece),
        out_shape=(
            jax.ShapeDtypeStruct((islands, 8, width), F32),
            jax.ShapeDtypeStruct((rows, mid), F32),
            jax.ShapeDtypeStruct((rows, mid), F32),
        ),
        in_specs=[SMEM, SMEM] + [VMEM] * (4 + chips - 1),
        out_specs=(VMEM, VMEM, VMEM),
        scratch_shapes=[pltpu.VMEM((8, mid), F32)],
        compiler_params=PARAMS,
        name="pack",
    )(where, mine[None], run_long[-1], run_short[-1], short[-1], q_t, *run_long, *run_short)
    got_rows = lax.ppermute(given, "fsdp", swap)
    mean = jnp.sum(lax.all_to_all(sent, "dp", 0, 0, tiled=True), axis=0)
    mean, got_rows = lax.optimization_barrier((mean, got_rows))
    mean = lax.all_to_all(jnp.broadcast_to(mean[None], (groups, 8, width)), "fsdp", 0, 0, tiled=True)
    sent = pl.pallas_call(
        functools.partial(factor_kernel, piece),
        out_shape=jax.ShapeDtypeStruct((islands, 8, width + LANES), F32),
        in_specs=[SMEM, VMEM],
        out_specs=VMEM,
        compiler_params=PARAMS,
        name="factor",
    )(where, mean)
    got = lax.all_to_all(sent, "dp", 0, 0, tiled=True)
    error_out, approx, q_next = pl.pallas_call(
        functools.partial(unpack_kernel, piece),
        out_shape=(
            jax.ShapeDtypeStruct((rows, f_blk), F32),
            jax.ShapeDtypeStruct((rows, cols), F32),
            jax.ShapeDtypeStruct((rank, own_q), F32),
        ),
        in_specs=[SMEM, VMEM, VMEM, VMEM],
        out_specs=(VMEM, VMEM, VMEM),
        scratch_shapes=[pltpu.VMEM((8, mid), F32)],
        compiler_params=PARAMS,
        name="unpack",
    )(where, got, kept, got_rows)
    return (error_out[None], approx, q_next.T)


def solution(mesh):
    return jax.shard_map(
        shards,
        mesh=mesh,
        in_specs=(
            P("dp", "fsdp", None),
            P("dp", "fsdp", None),
            P("dp", "fsdp", None),
            P("fsdp", None),
            P(),
            P(),
        ),
        out_specs=(P("dp", "fsdp", None), P("fsdp", "dp"), P("fsdp", None)),
        check_vma=False,
    )
```

```python
import functools

import jax
import jax.numpy as jnp
from jax import lax
from jax.experimental import pallas as pl
from jax.experimental.pallas import tpu as pltpu
from jax.sharding import PartitionSpec as P

HIGHEST = lax.Precision.HIGHEST
LANES = 128
SLOT = 32
F32 = jnp.float32


def iota(shape, axis):
    return lax.broadcasted_iota(jnp.int32, shape, axis)


def contract(x, z, dims):
    return lax.dot_general(x, z, ((dims[:1], dims[1:]), ((), ())), precision=HIGHEST, preferred_element_type=F32)


def product_kernel(splits, where_ref, a_ref, c_ref, error_ref, *refs):
    *out_refs, held_ref, sems = refs
    side = where_ref[0]
    span = error_ref.shape[1] // (2 * sems.shape[0])
    starts = [pl.multiple_of((2 * j + side) * span, LANES) for j in range(sems.shape[0])]
    copies = []
    for j, at in enumerate(starts):
        copies.append(pltpu.make_async_copy(c_ref.at[:, pl.ds(at, span)], held_ref.at[:, j * span : (j + 1) * span], sems.at[j]))
        copies[j].start()
    chunk = error_ref.shape[0]
    a = a_ref[...]
    for j in range(0, len(copies), 2):
        copies[j].wait()
        copies[j + 1].wait()
        cols = slice(j * span, (j + 2) * span)
        out = jnp.dot(a, held_ref[:, cols], preferred_element_type=F32)
        last = out[-chunk:] + jnp.concatenate([error_ref[:, pl.ds(at, span)] for at in starts[j : j + 2]], axis=1)
        first = 0
        for n, size in enumerate(splits):
            if n < len(splits) - 1:
                out_refs[n][:, cols] = out[first : first + size]
            else:
                if size > chunk:
                    out_refs[n][: size - chunk, cols] = out[first : first + size - chunk]
                out_refs[n][size - chunk :, cols] = last
            first += size


def step_kernel(came_ref, own_ref, got_ref, out_ref):
    mid = own_ref.shape[1]
    out_ref[:, :mid] = came_ref[:, :mid] + (own_ref[...] + got_ref[...])
    out_ref[:, mid:] = came_ref[:, mid:]


def pack_kernel(n_dp, piece, where_ref, mine_ref, long_ref, short_ref, own_ref, q_ref, *refs):
    *shard_refs, sent_ref, kept_ref, given_ref, sum_ref = refs
    y, core = where_ref[0], where_ref[1]
    chips, span = len(shard_refs) + 1, q_ref.shape[1]
    mid = own_ref.shape[1]
    total = long_ref[:, :mid] + short_ref[:, :mid] + own_ref[...]
    sum_ref[...] = total
    upper, lower = total[:4], total[4:]
    kept_ref[...] = jnp.where(core == 0, upper, lower)
    given_ref[...] = jnp.where(core == 0, lower, upper)

    rank = q_ref.shape[0]
    parts = jnp.zeros((8, rank), F32)
    for k in range(chips):
        if k == 0:
            shard, chip = q_ref[...], y
        else:
            held = shard_refs[k - 1][:, mid:]
            shard = jnp.concatenate([held[:, a * span : (a + 1) * span] for a in range(rank // 8)], axis=0)
            step = k if k <= chips // 2 else chips // 2 - k
            chip = lax.rem(y + chips - jnp.where(core == 0, step, -step), chips)
        start = pl.multiple_of(chip * span, LANES)
        parts = parts + contract(sum_ref[:, pl.ds(start, span)], shard, (1, 1))

    mine = mine_ref[0]
    scaled = total * mine

    slots = mid // span
    width = slots * SLOT
    spot = (iota((rank, width), 1) // SLOT) * (SLOT - piece) + iota((rank, width), 1) % SLOT - piece
    place = ((iota((rank, width), 1) % SLOT >= piece) & (spot == iota((rank, width), 0))).astype(F32)
    base = contract(parts * mine, place, (1, 0))
    lane = iota((8, LANES), 1)
    for k in range(n_dp):
        first = (k * piece) // LANES
        for v in range(width // LANES):
            out = base[:, v * LANES : (v + 1) * LANES]
            for b in range(LANES // SLOT):
                f = v * (LANES // SLOT) + b
                for w in range(first, (k * piece + piece - 1) // LANES + 1):
                    src = f * span + w * LANES
                    at = k * piece - w * LANES
                    moved = pltpu.roll(scaled[:, src : src + LANES], (b * SLOT - at) % LANES, 1)
                    lo = b * SLOT + max(0, -at)
                    hi = b * SLOT + min(piece, LANES - at)
                    out = jnp.where((lane >= lo) & (lane < hi), moved, out)
            sent_ref[k, :, v * LANES : (v + 1) * LANES] = out


def factor_kernel(piece, where_ref, mean_ref, sent_ref):
    f = where_ref[3]
    groups, _, width = mean_ref.shape
    slots = width // SLOT
    rank = slots * (SLOT - piece)
    d_blk = groups * 4
    mean = mean_ref[...].reshape(groups * 8, width)
    lane_i, sub_i = iota((width, LANES), 0), iota((width, LANES), 1)
    pick = ((lane_i % SLOT >= piece) & ((lane_i // SLOT) * (SLOT - piece) + lane_i % SLOT - piece == sub_i)).astype(F32)
    p_all = contract(mean, pick, (1, 0)).reshape(groups // 2, 2, 8, LANES)
    p_sum = (p_all[:, 0] + p_all[:, 1]).reshape(d_blk, LANES)

    sub, lane = iota((d_blk, LANES), 0), iota((d_blk, LANES), 1)
    wide = p_sum + (lane == sub + rank).astype(F32)
    a = contract(p_sum, wide, (0, 0))[:rank]
    row_i = iota((rank, LANES), 0)
    for k in range(rank):
        pivot = a[k : k + 1, k : k + 1]
        inv = lax.rsqrt(pivot)
        inv = inv * (1.5 - 0.5 * pivot * inv * inv)
        row = a[k : k + 1, :] * inv
        col = jnp.where(row_i[:, :1] > k, a[:, k : k + 1] * inv, 0.0)
        a = jnp.where(row_i == k, row, a - col * row)

    approx = jnp.zeros((8, width), F32)
    halves = []
    src, dst = iota((LANES, groups * 8), 0) - rank, iota((LANES, groups * 8), 1)
    for h in range(2):
        spread = ((dst // 8 % 2 == h) & (src == dst // 16 * 8 + dst % 8)).astype(F32)
        q_half = contract(contract(a, spread, (1, 0)), mean, (1, 0))
        own = ((iota((LANES, 8), 1) // 4 == h) & (iota((LANES, 8), 0) - rank == f * 4 + iota((LANES, 8), 1) % 4)).astype(F32)
        approx = approx + contract(contract(a, own, (1, 0)), q_half, (0, 0))
        halves.append(q_half)
    q_mine = jnp.where(lax.rem(f, 2) == 0, halves[0], halves[1])
    q_mine = pltpu.roll(q_mine, lax.rem(width - f // 2 * SLOT, width), 1)[:, :LANES]
    lane = iota((8, LANES), 1)
    q_out = jnp.zeros((8, LANES), F32)
    for b in range(rank // 8):
        q_out = jnp.where(lane // SLOT == b, pltpu.roll(q_mine[b * 8 : b * 8 + 8], b * SLOT, 1), q_out)
    for k in range(sent_ref.shape[0]):
        sent_ref[k, :, :width] = approx
        sent_ref[k, :, width:] = q_out


def unpack_kernel(piece, where_ref, got_ref, kept_ref, got_row_ref, error_ref, approx_ref, q_ref, whole_ref):
    i, core = where_ref[2], where_ref[1]
    n_dp, _, width = got_ref.shape
    width -= LANES
    span = q_ref.shape[1]
    slots = width // SLOT
    lane = iota((8, LANES), 1)
    for f in range(slots):
        v, b = f * SLOT // LANES, f % (LANES // SLOT)
        for w in range(span // LANES):
            out = jnp.zeros((8, LANES), F32)
            for k in range(w * LANES // piece, ((w + 1) * LANES - 1) // piece + 1):
                at = k * piece - w * LANES
                moved = pltpu.roll(got_ref[k, :, v * LANES : (v + 1) * LANES], (at - b * SLOT) % LANES, 1)
                out = jnp.where((lane >= at) & (lane < at + piece), moved, out)
            whole_ref[:, f * span + w * LANES : f * span + (w + 1) * LANES] = out
    for b in range(q_ref.shape[0] // 8):
        for w in range(span // LANES):
            out = jnp.zeros((8, LANES), F32)
            for k in range(w * LANES // piece, ((w + 1) * LANES - 1) // piece + 1):
                at = k * piece - w * LANES
                moved = pltpu.roll(got_ref[k, :, width:], (at - b * SLOT) % LANES, 1)
                out = jnp.where((lane >= at) & (lane < at + piece), moved, out)
            q_ref[b * 8 : b * 8 + 8, w * LANES : (w + 1) * LANES] = out
    for f in range(2 * slots):
        h, at = f % 2, f // 2 * span
        merged = jnp.where(core == h, kept_ref[:, at : at + span], got_row_ref[:, at : at + span])
        error_ref[:, f * span : (f + 1) * span] = merged - whole_ref[4 * h : 4 * h + 4, at : at + span]
    cols = approx_ref.shape[1]
    f, odd = i // 2, lax.rem(i, 2)
    start = pl.multiple_of(f // 2 * span + odd * (cols // LANES * LANES), LANES)
    window = whole_ref[:, pl.ds(start, cols + LANES // 2)]
    window = jnp.where(odd == 0, window, pltpu.roll(window, cols, 1))
    window = jnp.where(lax.rem(f, 2) == 0, window[:4], window[4:])
    approx_ref[...] = window[:, :cols]


VMEM = pl.BlockSpec(memory_space=pltpu.VMEM)
SMEM = pl.BlockSpec(memory_space=pltpu.SMEM)
PARAMS = pltpu.CompilerParams(vmem_limit_bytes=8 * 2**20)


def shards(acts, cot, error_in, q_warm, quorum, counts):
    groups = lax.axis_size("fsdp")
    islands = lax.axis_size("dp")
    chips = groups // 2
    f = lax.axis_index("fsdp")
    i = lax.axis_index("dp")
    y, core = f // 2, f % 2
    a, c = acts[0], cot[0]
    own_q, rank = q_warm.shape
    d_blk, f_blk = a.shape[1], c.shape[1]
    rows = d_blk // groups
    chunk = 2 * rows
    half = chips // 2
    cols = f_blk // islands
    piece = own_q // islands
    mid = f_blk // 2

    weight = (quorum * counts).astype(F32)
    total = jnp.sum(weight)
    mine = jnp.sum(jnp.where(jnp.arange(islands) == i, weight, 0.0)) / total

    swap = [(k, k ^ 1) for k in range(groups)]
    rise = [(2 * k, 2 * ((k + 1) % chips)) for k in range(chips)] + [(2 * k + 1, 2 * ((k - 1) % chips) + 1) for k in range(chips)]
    fall = [(k, j) for j, k in rise]
    where = jnp.stack([y, core, i, f])
    block = jnp.arange(d_blk) // chunk
    ahead = jnp.where(block < half, half - block, block - (chips - 1))

    place = jnp.arange(chunk)[:, None] // rows == core
    errors = jnp.where(place, jnp.concatenate([error_in[0], error_in[0]], axis=0), 0.0)

    def product(side, splits, limit):
        picked = (y + jnp.where(side == 0, ahead, -ahead)) % chips * chunk + jnp.arange(d_blk) % chunk
        onehot = (picked[:, None] == jnp.arange(d_blk)[None, :]).astype(a.dtype)
        chosen = jnp.einsum("nd,td->nt", onehot, a, preferred_element_type=F32).astype(a.dtype)
        return pl.pallas_call(
            functools.partial(product_kernel, splits),
            out_shape=[pltpu.VMEM((size, mid), F32) for size in splits],
            in_specs=[SMEM, VMEM, pl.BlockSpec(memory_space=pl.ANY), VMEM],
            out_specs=[VMEM] * len(splits),
            scratch_shapes=[pltpu.VMEM((c.shape[0], mid), c.dtype), pltpu.SemaphoreType.DMA((chips,))],
            compiler_params=pltpu.CompilerParams(vmem_limit_bytes=limit * 2**20),
            name="product",
        )(side[None], chosen, c, errors)

    other_long, other_short = product(1 - core, (half * chunk, half * chunk), 6)
    far, *own = product(core, (chunk,) * chips, 6)
    got_long = lax.ppermute(other_long, "fsdp", swap)
    got_short = lax.ppermute(other_short, "fsdp", swap)
    far = far + got_long[:chunk]
    long = [own[k] + got_long[(k + 1) * chunk : (k + 2) * chunk] for k in range(half - 1)]
    short = [own[half - 1 + k] + got_short[k * chunk : (k + 1) * chunk] for k in range(half)]

    q_t = q_warm.T
    held = q_t.reshape(rank // 8, 8, own_q).transpose(1, 0, 2).reshape(8, rank // 8 * own_q)
    run_long = [lax.ppermute(jnp.concatenate([far, held], axis=1), "fsdp", rise)]
    run_short = []
    for k in range(half - 1):
        last = run_long[-1]
        start = jnp.concatenate([last[:, :mid] + long[k], last[:, mid:]], axis=1)
        if k == half - 2:
            start = pl.pallas_call(
                step_kernel,
                out_shape=pltpu.VMEM(start.shape, F32),
                in_specs=[VMEM] * 3,
                out_specs=VMEM,
                compiler_params=pltpu.CompilerParams(vmem_limit_bytes=4 * 2**20),
                name="step",
            )(last, own[k], got_long[half * chunk - chunk :])
        run_long.append(lax.ppermute(start, "fsdp", rise))
        if k == 0:
            last = jnp.concatenate([short[0], held], axis=1)
        else:
            last = jnp.concatenate([run_short[-1][:, :mid] + short[k], run_short[-1][:, mid:]], axis=1)
        run_short.append(lax.ppermute(last, "fsdp", fall))

    width = mid // own_q * SLOT
    sent, kept, given = pl.pallas_call(
        functools.partial(pack_kernel, islands, piece),
        out_shape=(
            jax.ShapeDtypeStruct((islands, 8, width), F32),
            jax.ShapeDtypeStruct((rows, mid), F32),
            jax.ShapeDtypeStruct((rows, mid), F32),
        ),
        in_specs=[SMEM, SMEM] + [VMEM] * (4 + chips - 1),
        out_specs=(VMEM, VMEM, VMEM),
        scratch_shapes=[pltpu.VMEM((8, mid), F32)],
        compiler_params=PARAMS,
        name="pack",
    )(where, mine[None], run_long[-1], run_short[-1], short[-1], q_t, *run_long, *run_short)
    got_rows = lax.ppermute(given, "fsdp", swap)
    mean = jnp.sum(lax.all_to_all(sent, "dp", 0, 0, tiled=True), axis=0)
    mean, got_rows = lax.optimization_barrier((mean, got_rows))
    mean = lax.all_to_all(jnp.broadcast_to(mean[None], (groups, 8, width)), "fsdp", 0, 0, tiled=True)
    sent = pl.pallas_call(
        functools.partial(factor_kernel, piece),
        out_shape=jax.ShapeDtypeStruct((islands, 8, width + LANES), F32),
        in_specs=[SMEM, VMEM],
        out_specs=VMEM,
        compiler_params=PARAMS,
        name="factor",
    )(where, mean)
    got = lax.all_to_all(sent, "dp", 0, 0, tiled=True)
    error_out, approx, q_next = pl.pallas_call(
        functools.partial(unpack_kernel, piece),
        out_shape=(
            jax.ShapeDtypeStruct((rows, f_blk), F32),
            jax.ShapeDtypeStruct((rows, cols), F32),
            jax.ShapeDtypeStruct((rank, own_q), F32),
        ),
        in_specs=[SMEM, VMEM, VMEM, VMEM],
        out_specs=(VMEM, VMEM, VMEM),
        scratch_shapes=[pltpu.VMEM((8, mid), F32)],
        compiler_params=PARAMS,
        name="unpack",
    )(where, got, kept, got_rows)
    return (error_out[None], approx, q_next.T)


def solution(mesh):
    return jax.shard_map(
        shards,
        mesh=mesh,
        in_specs=(
            P("dp", "fsdp", None),
            P("dp", "fsdp", None),
            P("dp", "fsdp", None),
            P("fsdp", None),
            P(),
            P(),
        ),
        out_specs=(P("dp", "fsdp", None), P("fsdp", "dp"), P("fsdp", None)),
        check_vma=False,
    )
```

```python
import functools

import jax
import jax.numpy as jnp
from jax import lax
from jax.experimental import pallas as pl
from jax.experimental.pallas import tpu as pltpu
from jax.sharding import PartitionSpec as P

HIGHEST = lax.Precision.HIGHEST
LANES = 128
SLOT = 32
F32 = jnp.float32


def iota(shape, axis):
    return lax.broadcasted_iota(jnp.int32, shape, axis)


def contract(x, z, dims):
    return lax.dot_general(x, z, ((dims[:1], dims[1:]), ((), ())), precision=HIGHEST, preferred_element_type=F32)


def product_kernel(splits, where_ref, a_ref, c_ref, error_ref, *refs):
    *out_refs, held_ref, sems = refs
    side = where_ref[0]
    span = error_ref.shape[1] // (2 * sems.shape[0])
    starts = [pl.multiple_of((2 * j + side) * span, LANES) for j in range(sems.shape[0])]
    copies = []
    for j, at in enumerate(starts):
        copies.append(pltpu.make_async_copy(c_ref.at[:, pl.ds(at, span)], held_ref.at[:, j * span : (j + 1) * span], sems.at[j]))
        copies[j].start()
    chunk = error_ref.shape[0]
    a = a_ref[...]
    for j in range(0, len(copies), 2):
        copies[j].wait()
        copies[j + 1].wait()
        cols = slice(j * span, (j + 2) * span)
        out = jnp.dot(a, held_ref[:, cols], preferred_element_type=F32)
        last = out[-chunk:] + jnp.concatenate([error_ref[:, pl.ds(at, span)] for at in starts[j : j + 2]], axis=1)
        first = 0
        for n, size in enumerate(splits):
            if n < len(splits) - 1:
                out_refs[n][:, cols] = out[first : first + size]
            else:
                if size > chunk:
                    out_refs[n][: size - chunk, cols] = out[first : first + size - chunk]
                out_refs[n][size - chunk :, cols] = last
            first += size


def step_kernel(came_ref, own_ref, got_ref, out_ref):
    mid = own_ref.shape[1]
    out_ref[:, :mid] = came_ref[:, :mid] + (own_ref[...] + got_ref[...])
    out_ref[:, mid:] = came_ref[:, mid:]


def pack_kernel(n_dp, piece, where_ref, mine_ref, long_ref, short_ref, own_ref, q_ref, *refs):
    *shard_refs, sent_ref, kept_ref, given_ref, sum_ref = refs
    y, core = where_ref[0], where_ref[1]
    chips, span = len(shard_refs) + 1, q_ref.shape[1]
    mid = own_ref.shape[1]
    total = long_ref[:, :mid] + short_ref[:, :mid] + own_ref[...]
    sum_ref[...] = total
    upper, lower = total[:4], total[4:]
    kept_ref[...] = jnp.where(core == 0, upper, lower)
    given_ref[...] = jnp.where(core == 0, lower, upper)

    rank = q_ref.shape[0]
    parts = jnp.zeros((8, rank), F32)
    for k in range(chips):
        if k == 0:
            shard, chip = q_ref[...], y
        else:
            held = shard_refs[k - 1][:, mid:]
            shard = jnp.concatenate([held[:, a * span : (a + 1) * span] for a in range(rank // 8)], axis=0)
            step = k if k <= chips // 2 else chips // 2 - k
            chip = lax.rem(y + chips - jnp.where(core == 0, -step, step), chips)
        start = pl.multiple_of(chip * span, LANES)
        parts = parts + contract(sum_ref[:, pl.ds(start, span)], shard, (1, 1))

    mine = mine_ref[0]
    scaled = total * mine

    slots = mid // span
    width = slots * SLOT
    spot = (iota((rank, width), 1) // SLOT) * (SLOT - piece) + iota((rank, width), 1) % SLOT - piece
    place = ((iota((rank, width), 1) % SLOT >= piece) & (spot == iota((rank, width), 0))).astype(F32)
    base = contract(parts * mine, place, (1, 0))
    lane = iota((8, LANES), 1)
    for k in range(n_dp):
        first = (k * piece) // LANES
        for v in range(width // LANES):
            out = base[:, v * LANES : (v + 1) * LANES]
            for b in range(LANES // SLOT):
                f = v * (LANES // SLOT) + b
                for w in range(first, (k * piece + piece - 1) // LANES + 1):
                    src = f * span + w * LANES
                    at = k * piece - w * LANES
                    moved = pltpu.roll(scaled[:, src : src + LANES], (b * SLOT - at) % LANES, 1)
                    lo = b * SLOT + max(0, -at)
                    hi = b * SLOT + min(piece, LANES - at)
                    out = jnp.where((lane >= lo) & (lane < hi), moved, out)
            sent_ref[k, :, v * LANES : (v + 1) * LANES] = out


def factor_kernel(piece, where_ref, mean_ref, sent_ref):
    f = where_ref[3]
    groups, _, width = mean_ref.shape
    slots = width // SLOT
    rank = slots * (SLOT - piece)
    d_blk = groups * 4
    mean = mean_ref[...].reshape(groups * 8, width)
    lane_i, sub_i = iota((width, LANES), 0), iota((width, LANES), 1)
    pick = ((lane_i % SLOT >= piece) & ((lane_i // SLOT) * (SLOT - piece) + lane_i % SLOT - piece == sub_i)).astype(F32)
    p_all = contract(mean, pick, (1, 0)).reshape(groups // 2, 2, 8, LANES)
    p_sum = (p_all[:, 0] + p_all[:, 1]).reshape(d_blk, LANES)

    sub, lane = iota((d_blk, LANES), 0), iota((d_blk, LANES), 1)
    wide = p_sum + (lane == sub + rank).astype(F32)
    a = contract(p_sum, wide, (0, 0))[:rank]
    row_i = iota((rank, LANES), 0)
    for k in range(rank):
        pivot = a[k : k + 1, k : k + 1]
        inv = lax.rsqrt(pivot)
        inv = inv * (1.5 - 0.5 * pivot * inv * inv)
        row = a[k : k + 1, :] * inv
        col = jnp.where(row_i[:, :1] > k, a[:, k : k + 1] * inv, 0.0)
        a = jnp.where(row_i == k, row, a - col * row)

    approx = jnp.zeros((8, width), F32)
    halves = []
    src, dst = iota((LANES, groups * 8), 0) - rank, iota((LANES, groups * 8), 1)
    for h in range(2):
        spread = ((dst // 8 % 2 == h) & (src == dst // 16 * 8 + dst % 8)).astype(F32)
        q_half = contract(contract(a, spread, (1, 0)), mean, (1, 0))
        own = ((iota((LANES, 8), 1) // 4 == h) & (iota((LANES, 8), 0) - rank == f * 4 + iota((LANES, 8), 1) % 4)).astype(F32)
        approx = approx + contract(contract(a, own, (1, 0)), q_half, (0, 0))
        halves.append(q_half)
    q_mine = jnp.where(lax.rem(f, 2) == 0, halves[0], halves[1])
    q_mine = pltpu.roll(q_mine, lax.rem(width - f // 2 * SLOT, width), 1)[:, :LANES]
    lane = iota((8, LANES), 1)
    q_out = jnp.zeros((8, LANES), F32)
    for b in range(rank // 8):
        q_out = jnp.where(lane // SLOT == b, pltpu.roll(q_mine[b * 8 : b * 8 + 8], b * SLOT, 1), q_out)
    for k in range(sent_ref.shape[0]):
        sent_ref[k, :, :width] = approx
        sent_ref[k, :, width:] = q_out


def unpack_kernel(piece, where_ref, got_ref, kept_ref, got_row_ref, error_ref, approx_ref, q_ref, whole_ref):
    i, core = where_ref[2], where_ref[1]
    n_dp, _, width = got_ref.shape
    width -= LANES
    span = q_ref.shape[1]
    slots = width // SLOT
    lane = iota((8, LANES), 1)
    for f in range(slots):
        v, b = f * SLOT // LANES, f % (LANES // SLOT)
        for w in range(span // LANES):
            out = jnp.zeros((8, LANES), F32)
            for k in range(w * LANES // piece, ((w + 1) * LANES - 1) // piece + 1):
                at = k * piece - w * LANES
                moved = pltpu.roll(got_ref[k, :, v * LANES : (v + 1) * LANES], (at - b * SLOT) % LANES, 1)
                out = jnp.where((lane >= at) & (lane < at + piece), moved, out)
            whole_ref[:, f * span + w * LANES : f * span + (w + 1) * LANES] = out
    for b in range(q_ref.shape[0] // 8):
        for w in range(span // LANES):
            out = jnp.zeros((8, LANES), F32)
            for k in range(w * LANES // piece, ((w + 1) * LANES - 1) // piece + 1):
                at = k * piece - w * LANES
                moved = pltpu.roll(got_ref[k, :, width:], (at - b * SLOT) % LANES, 1)
                out = jnp.where((lane >= at) & (lane < at + piece), moved, out)
            q_ref[b * 8 : b * 8 + 8, w * LANES : (w + 1) * LANES] = out
    for f in range(2 * slots):
        h, at = f % 2, f // 2 * span
        merged = jnp.where(core == h, kept_ref[:, at : at + span], got_row_ref[:, at : at + span])
        error_ref[:, f * span : (f + 1) * span] = merged - whole_ref[4 * h : 4 * h + 4, at : at + span]
    cols = approx_ref.shape[1]
    f, odd = i // 2, lax.rem(i, 2)
    start = pl.multiple_of(f // 2 * span + odd * (cols // LANES * LANES), LANES)
    window = whole_ref[:, pl.ds(start, cols + LANES // 2)]
    window = jnp.where(odd == 0, window, pltpu.roll(window, cols, 1))
    window = jnp.where(lax.rem(f, 2) == 0, window[:4], window[4:])
    approx_ref[...] = window[:, :cols]


VMEM = pl.BlockSpec(memory_space=pltpu.VMEM)
SMEM = pl.BlockSpec(memory_space=pltpu.SMEM)
PARAMS = pltpu.CompilerParams(vmem_limit_bytes=8 * 2**20)


def shards(acts, cot, error_in, q_warm, quorum, counts):
    groups = lax.axis_size("fsdp")
    islands = lax.axis_size("dp")
    chips = groups // 2
    f = lax.axis_index("fsdp")
    i = lax.axis_index("dp")
    y, core = f // 2, f % 2
    a, c = acts[0], cot[0]
    own_q, rank = q_warm.shape
    d_blk, f_blk = a.shape[1], c.shape[1]
    rows = d_blk // groups
    chunk = 2 * rows
    half = chips // 2
    cols = f_blk // islands
    piece = own_q // islands
    mid = f_blk // 2

    weight = (quorum * counts).astype(F32)
    total = jnp.sum(weight)
    mine = jnp.sum(jnp.where(jnp.arange(islands) == i, weight, 0.0)) / total

    swap = [(k, k ^ 1) for k in range(groups)]
    rise = [(2 * k, 2 * ((k - 1) % chips)) for k in range(chips)] + [(2 * k + 1, 2 * ((k + 1) % chips) + 1) for k in range(chips)]
    fall = [(k, j) for j, k in rise]
    where = jnp.stack([y, core, i, f])
    block = jnp.arange(d_blk) // chunk
    ahead = jnp.where(block < half, half - block, block - (chips - 1))

    place = jnp.arange(chunk)[:, None] // rows == core
    errors = jnp.where(place, jnp.concatenate([error_in[0], error_in[0]], axis=0), 0.0)

    def product(side, splits, limit):
        picked = (y + jnp.where(side == 0, -ahead, ahead)) % chips * chunk + jnp.arange(d_blk) % chunk
        onehot = (picked[:, None] == jnp.arange(d_blk)[None, :]).astype(a.dtype)
        chosen = jnp.einsum("nd,td->nt", onehot, a, preferred_element_type=F32).astype(a.dtype)
        return pl.pallas_call(
            functools.partial(product_kernel, splits),
            out_shape=[pltpu.VMEM((size, mid), F32) for size in splits],
            in_specs=[SMEM, VMEM, pl.BlockSpec(memory_space=pl.ANY), VMEM],
            out_specs=[VMEM] * len(splits),
            scratch_shapes=[pltpu.VMEM((c.shape[0], mid), c.dtype), pltpu.SemaphoreType.DMA((chips,))],
            compiler_params=pltpu.CompilerParams(vmem_limit_bytes=limit * 2**20),
            name="product",
        )(side[None], chosen, c, errors)

    other_long, other_short = product(1 - core, (half * chunk, half * chunk), 6)
    far, *own = product(core, (chunk,) * chips, 6)
    got_long = lax.ppermute(other_long, "fsdp", swap)
    got_short = lax.ppermute(other_short, "fsdp", swap)
    far = far + got_long[:chunk]
    long = [own[k] + got_long[(k + 1) * chunk : (k + 2) * chunk] for k in range(half - 1)]
    short = [own[half - 1 + k] + got_short[k * chunk : (k + 1) * chunk] for k in range(half)]

    q_t = q_warm.T
    held = q_t.reshape(rank // 8, 8, own_q).transpose(1, 0, 2).reshape(8, rank // 8 * own_q)
    run_long = [lax.ppermute(jnp.concatenate([far, held], axis=1), "fsdp", rise)]
    run_short = []
    for k in range(half - 1):
        last = run_long[-1]
        start = jnp.concatenate([last[:, :mid] + long[k], last[:, mid:]], axis=1)
        if k == half - 2:
            start = pl.pallas_call(
                step_kernel,
                out_shape=pltpu.VMEM(start.shape, F32),
                in_specs=[VMEM] * 3,
                out_specs=VMEM,
                compiler_params=pltpu.CompilerParams(vmem_limit_bytes=4 * 2**20),
                name="step",
            )(last, own[k], got_long[half * chunk - chunk :])
        run_long.append(lax.ppermute(start, "fsdp", rise))
        if k == 0:
            last = jnp.concatenate([short[0], held], axis=1)
        else:
            last = jnp.concatenate([run_short[-1][:, :mid] + short[k], run_short[-1][:, mid:]], axis=1)
        run_short.append(lax.ppermute(last, "fsdp", fall))

    width = mid // own_q * SLOT
    sent, kept, given = pl.pallas_call(
        functools.partial(pack_kernel, islands, piece),
        out_shape=(
            jax.ShapeDtypeStruct((islands, 8, width), F32),
            jax.ShapeDtypeStruct((rows, mid), F32),
            jax.ShapeDtypeStruct((rows, mid), F32),
        ),
        in_specs=[SMEM, SMEM] + [VMEM] * (4 + chips - 1),
        out_specs=(VMEM, VMEM, VMEM),
        scratch_shapes=[pltpu.VMEM((8, mid), F32)],
        compiler_params=PARAMS,
        name="pack",
    )(where, mine[None], run_long[-1], run_short[-1], short[-1], q_t, *run_long, *run_short)
    got_rows = lax.ppermute(given, "fsdp", swap)
    mean = jnp.sum(lax.all_to_all(sent, "dp", 0, 0, tiled=True), axis=0)
    mean, got_rows = lax.optimization_barrier((mean, got_rows))
    mean = lax.all_to_all(jnp.broadcast_to(mean[None], (groups, 8, width)), "fsdp", 0, 0, tiled=True)
    sent = pl.pallas_call(
        functools.partial(factor_kernel, piece),
        out_shape=jax.ShapeDtypeStruct((islands, 8, width + LANES), F32),
        in_specs=[SMEM, VMEM],
        out_specs=VMEM,
        compiler_params=PARAMS,
        name="factor",
    )(where, mean)
    got = lax.all_to_all(sent, "dp", 0, 0, tiled=True)
    error_out, approx, q_next = pl.pallas_call(
        functools.partial(unpack_kernel, piece),
        out_shape=(
            jax.ShapeDtypeStruct((rows, f_blk), F32),
            jax.ShapeDtypeStruct((rows, cols), F32),
            jax.ShapeDtypeStruct((rank, own_q), F32),
        ),
        in_specs=[SMEM, VMEM, VMEM, VMEM],
        out_specs=(VMEM, VMEM, VMEM),
        scratch_shapes=[pltpu.VMEM((8, mid), F32)],
        compiler_params=PARAMS,
        name="unpack",
    )(where, got, kept, got_rows)
    return (error_out[None], approx, q_next.T)


def solution(mesh):
    return jax.shard_map(
        shards,
        mesh=mesh,
        in_specs=(
            P("dp", "fsdp", None),
            P("dp", "fsdp", None),
            P("dp", "fsdp", None),
            P("fsdp", None),
            P(),
            P(),
        ),
        out_specs=(P("dp", "fsdp", None), P("fsdp", "dp"), P("fsdp", None)),
        check_vma=False,
    )
```
